128 devices in a mesh: prow: 8 (over z, core), pcol: 16 (over x, y).
Axes of the slice: x: 4, y: 4, z: 4, core: 2. Of those that a mesh axis runs over, the one named last changes fastest.
Arguments:
- matrix: float32 [6, 8, 256, 3, 16, 256], P(None, 'prow', None, None, 'pcol'), may hold values from -6 to 6
- row_order: int32 [12288], replicated, may hold values from 0 to 12287, as said below
- inverses: float32 [4, 256, 256], replicated, may hold values from -0.0234375 to 0.0234375
- lower_fill: int32 [4, 48], replicated, may hold values 0 or 1
- upper_fill: int32 [4, 48], replicated, may hold values 0 or 1
Outputs:
- factored: float32 [6, 8, 256, 3, 16, 256], P(None, 'prow', None, None, 'pcol')
The draws below stay inside these ranges and needn't reach their ends.
Inputs may be any that keep to these rules, and one draw needn't show every extreme that they name: row_order is a permutation of the rows; of the rows whose block row index is congruent to p modulo the number of indices of prow, exactly 6 * 256 divided by that number go to rows whose block row index is congruent to s, for every p and s.
All inputs are finite; a program needn't handle non-finite values.
Results may differ from the reference program's by a relative error of at most 0.0002.
Values sent between devices are 32-bit elements; how exact they have to be, the bound alone decides.
No kernel may reach another device: no remote copies, remote signals or barrier semaphores. Data moves between devices by JAX's collectives and lax.ppermute only.
A program may use at most 128 MiB of HBM per device.

```python
import jax
import jax.numpy as jnp
from jax import lax

B = 256
CB = 3
PANELS = 4
RB = 6
NB = 48
N_PROW = 8
N_PCOL = 16


def draw_row_order(key, part):
    local_rows = RB * B
    share = local_rows // N_PROW
    offsets = jnp.arange(local_rows, dtype=jnp.int32)
    owners = jnp.arange(N_PROW, dtype=jnp.int32)
    rows = (offsets[None, :] // B * N_PROW + owners[:, None]) * B + offsets[None, :] % B
    first, second = jax.random.split(jax.random.fold_in(key, 11))

    def shuffle(subkey):
        return jax.vmap(lambda single: jax.random.permutation(single, local_rows))(jax.random.split(subkey, N_PROW))
    sources = jnp.take_along_axis(rows, shuffle(first), 1).reshape(N_PROW, N_PROW, share)
    targets = jnp.take_along_axis(rows, shuffle(second), 1).reshape(N_PROW, N_PROW, share)
    moved = jnp.transpose(targets, (1, 0, 2)).reshape(-1)
    return jnp.zeros((NB * B,), jnp.int32).at[sources.reshape(-1)].set(moved)


def set_ends(values, stream_key, least, top_value):
    dims = values.shape
    place = [jax.random.randint(jax.random.fold_in(stream_key, axis), (), 0, dims[axis]) for axis in range(len(dims))]
    values = values.at[tuple(place)].set(least)
    longest = dims.index(max(dims))
    place[longest] = (place[longest] + 1) % dims[longest]
    return values.at[tuple(place)].set(top_value)


def shard_levels(rng, extent, cuts, least, top_value):
    level, own = 1.0, jax.random.fold_in(rng, 6)
    for position, shards_of in cuts:
        steps = jnp.exp(jax.random.uniform(jax.random.fold_in(own, position), (shards_of,), jnp.float32, least / len(cuts), top_value / len(cuts)))
        level = level * jnp.repeat(steps, extent[position] // shards_of).reshape([-1 if axis == position else 1 for axis in range(len(extent))])
    return level


def bell_draw(own_key, shape, spread, reach, pieces=(), kind=jnp.bfloat16):
    factor_of = shard_levels(own_key, shape, pieces, -0.22, 0.18) if pieces else 1.0
    entries = jax.random.normal(own_key, shape, jnp.float32) * spread * factor_of
    return jnp.minimum(jnp.maximum(entries, -reach), reach).astype(kind)


def setup_inputs(seed: int = 0) -> dict:
    streams_of = jax.random.split(jax.random.key(seed), 6)
    matrix = bell_draw(streams_of[0], (RB, N_PROW, B, CB, N_PCOL, B), 1.0, 6.0, ((1, 8), (4, 16)), jnp.float32)
    row_order = draw_row_order(jax.random.fold_in(streams_of[5], 71), 0)
    inverses = bell_draw(streams_of[2], (PANELS, B, B), (B * B) ** -0.5, 0.0234375, (), jnp.float32)
    lower_fill = set_ends((jax.random.randint(streams_of[3], (PANELS, NB), 0, 4) < 3).astype(jnp.int32), jax.random.fold_in(streams_of[3], 1), 0, 1)
    upper_fill = set_ends((jax.random.randint(streams_of[4], (PANELS, NB), 0, 4) < 3).astype(jnp.int32), jax.random.fold_in(streams_of[4], 1), 0, 1)
    return dict(matrix=matrix, row_order=row_order, inverses=inverses, lower_fill=lower_fill, upper_fill=upper_fill)


def reference(matrix, row_order, inverses, lower_fill, upper_fill):
    order_n = NB * B
    whole = matrix.reshape(order_n, order_n)
    work = jnp.zeros_like(whole).at[row_order].set(whole)
    blocks = jnp.arange(NB, dtype=jnp.int32)
    for k in range(PANELS):
        keep_rows = jnp.repeat(((blocks > k) & (lower_fill[k] == 1)).astype(jnp.float32), B)
        keep_cols = jnp.repeat(((blocks > k) & (upper_fill[k] == 1)).astype(jnp.float32), B)
        column = work[:, k * B:(k + 1) * B]
        lower = jnp.dot(column, inverses[k], precision=lax.Precision.HIGHEST, preferred_element_type=jnp.float32) * keep_rows[:, None]
        upper = work[k * B:(k + 1) * B, :] * keep_cols[None, :]
        start = (k + 1) * B
        update = jnp.dot(lower[start:], upper[:, start:], precision=lax.Precision.HIGHEST, preferred_element_type=jnp.float32)
        work = work.at[start:, start:].add(-update)
        work = work.at[start:, k * B:(k + 1) * B].set(lower[start:])
    return work.reshape(RB, N_PROW, B, CB, N_PCOL, B)
```

```python
import jax
import jax.numpy as jnp
from jax import lax
from jax.experimental import pallas as pl
from jax.experimental.pallas import tpu as pltpu
from jax.sharding import PartitionSpec as P

HIGH = lax.Precision.HIGH
VMEM = pl.BlockSpec(memory_space=pltpu.VMEM)
SMEM = pl.BlockSpec(memory_space=pltpu.SMEM)
PARAMS = pltpu.CompilerParams(vmem_limit_bytes=48 * 1024 * 1024)


def dot(a, b):
    return jnp.dot(a, b, precision=HIGH, preferred_element_type=jnp.float32)


def send_kernel(order, x, first, rest):
    def step(j, carry):
        r = order[j] * 3
        first[j] = x[r]
        rest[2 * j] = x[r + 1]
        rest[2 * j + 1] = x[r + 2]
        return carry

    lax.fori_loop(0, first.shape[0], step, 0, unroll=8)


def rows_kernel(order, first, rest, out):
    def step(d, carry):
        m = order[d]
        out[3 * d] = first[m]
        out[3 * d + 1] = rest[2 * m]
        out[3 * d + 2] = rest[2 * m + 1]
        return carry

    lax.fori_loop(0, out.shape[0] // 3, step, 0, unroll=8)


def f32(*shape):
    return jax.ShapeDtypeStruct(shape, jnp.float32)


def scatter_x(blocks, here_x):
    got = [
        lax.ppermute(blocks[s], "pcol", [(k, k + 4 * s) for k in range(4)]) for s in range(1, 4)
    ]
    return jnp.where(here_x == 0, blocks[0], got[0] + got[1] + got[2])


def body(matrix, row_order, inverses, lower_fill, upper_fill):
    here_row = lax.axis_index("prow")
    here_col = lax.axis_index("pcol")
    here_x = here_col // 4
    core = here_row % 2
    x = matrix.reshape(4608, 2, 128)
    targets = row_order.reshape(6, 8, 256).transpose(1, 0, 2).reshape(8, 1536)
    local = jnp.arange(1536, dtype=jnp.int32)

    def keys(t):
        owner, row = t // 256 % 8, t // 2048 * 256 + t % 256
        return (owner * 2048 + local) * 2048 + row

    mine = lax.dynamic_slice(targets, (here_row, 0), (1, 1536))[0]
    order = lax.sort(keys(mine)) // 2048 % 2048
    first, rest = pl.pallas_call(
        send_kernel,
        out_shape=(f32(1536, 2, 128), f32(3072, 2, 128)),
        in_specs=[SMEM, VMEM],
        out_specs=(VMEM, VMEM),
        compiler_params=PARAMS,
        name="send_rows",
    )(order, x)
    quarters = first.reshape(8, 4, 96, 128).transpose(1, 0, 2, 3)
    mine_q = scatter_x(quarters, here_x)
    mine_q = lax.all_to_all(mine_q, "prow", 0, 0, tiled=True).reshape(384, 256)
    got_first = lax.all_to_all(first.reshape(8, 384, 128), "prow", 0, 0, tiled=True)
    got_rest = lax.all_to_all(rest.reshape(8, 768, 128), "prow", 0, 0, tiled=True)
    all_keys = lax.sort(keys(targets), dimension=1)
    places = lax.dynamic_slice(all_keys, (0, here_row * 192), (8, 192)).reshape(1536) % 2048
    backward = lax.sort(places * 2048 + local) % 2048
    got_first = got_first.reshape(1536, 2, 128)
    got_rest = got_rest.reshape(3072, 2, 128)
    top = pl.pallas_call(
        rows_kernel,
        out_shape=f32(768, 2, 128),
        in_specs=[SMEM, VMEM, VMEM],
        out_specs=VMEM,
        compiler_params=PARAMS,
        name="top_rows",
    )(backward[:256], got_first, got_rest).reshape(256, 768)
    half = lax.ppermute(top[128:], "prow", [(p, p + 4) for p in range(4)])
    piece = jnp.where(here_row < 4, top[:128], half)
    rows = lax.all_gather(piece, "prow", axis=0, tiled=True).reshape(2, 4, 128, 768)
    rows = rows.transpose(1, 0, 2, 3).reshape(1024, 768)
    columns = lax.all_gather(mine_q, "pcol", axis=0, tiled=True)
    columns = columns.reshape(4, 4, 8, 48, 256).transpose(1, 2, 0, 3, 4).reshape(4, 1536, 256)
    corner = lax.dynamic_slice(rows, (core * 512, 0), (512, 256)).reshape(4, 128, 256)
    corner = lax.all_gather(scatter_x(corner, here_x), "pcol", axis=0, tiled=True)
    corner = corner.reshape(4, 4, 128, 256).transpose(1, 0, 2, 3).reshape(4, 512, 256)
    other = lax.ppermute(corner, "prow", [(p, p ^ 1) for p in range(8)])
    corner = jnp.where(core == 0, jnp.stack([corner, other]), jnp.stack([other, corner]))
    corner = corner.reshape(2, 4, 2, 256, 256)
    tl = [[corner[i // 2, j, i % 2] for j in range(4)] for i in range(4)]
    lf = (lower_fill == 1).astype(jnp.float32)
    uf = (upper_fill == 1).astype(jnp.float32)
    low, upp = {}, {}
    for k in range(4):
        for m in range(k):
            t = tl[k][m]
            for n in range(m):
                t = t - dot(low[k, n], upp[n, m])
            low[k, m] = dot(t, inverses[m]) * lf[m, k]
        for j in range(k + 1, 4):
            t = tl[k][j]
            for m in range(k):
                t = t - dot(low[k, m], upp[m, j])
            upp[k, j] = t * uf[k, j]
    blocks = jnp.arange(3, dtype=jnp.int32) * 16 + here_col
    upper = []
    for k in range(4):
        keep = jnp.where(blocks > k, uf[k][blocks], 0.0)
        t = rows[256 * k : 256 * k + 256]
        for m in range(k):
            t = t - dot(low[k, m], upper[m])
        upper.append(t * jnp.repeat(keep, 256)[None, :])
    row_block = places // 256 * 8 + here_row
    lower = []
    for k in range(4):
        keep6 = jnp.arange(6, dtype=jnp.int32) * 8 + here_row
        keep6 = jnp.where(keep6 > k, lf[k][keep6], 0.0)
        keep = jnp.zeros((1536,), jnp.float32)
        for r in range(6):
            keep = jnp.where(places // 256 == r, keep6[r], keep)
        t = columns[k]
        for m in range(k):
            t = t - dot(lower[m], upp[m, k])
        lower.append(dot(t, inverses[k]) * keep[:, None])
    lower = jnp.concatenate(lower, axis=1)
    upper = jnp.concatenate(upper, axis=0)
    done = dot(lower, upper)
    new_first = got_first.reshape(1536, 256) - done[:, :256]
    own = lax.dynamic_slice(lower, (0, jnp.minimum(here_col, 3) * 256), (1536, 256))
    new_first = jnp.where(((here_col < 4) & (row_block > here_col))[:, None], own, new_first)
    new_rest = got_rest.reshape(1536, 512) - done[:, 256:]
    out = pl.pallas_call(
        rows_kernel,
        out_shape=f32(4608, 2, 128),
        in_specs=[SMEM, VMEM, VMEM],
        out_specs=VMEM,
        compiler_params=PARAMS,
        name="place_rows",
    )(backward, new_first.reshape(1536, 2, 128), new_rest.reshape(3072, 2, 128))
    return out.reshape(6, 1, 256, 3, 1, 256)


def solution(mesh):
    in_specs = (P(None, "prow", None, None, "pcol", None), P(), P(), P(), P())
    out_specs = P(None, "prow", None, None, "pcol", None)
    return jax.shard_map(body, mesh=mesh, in_specs=in_specs, out_specs=out_specs, check_vma=False)
```

```python
import jax
import jax.numpy as jnp
from jax import lax
from jax.experimental import pallas as pl
from jax.experimental.pallas import tpu as pltpu
from jax.sharding import PartitionSpec as P

VMEM = pl.BlockSpec(memory_space=pltpu.VMEM)
SMEM = pl.BlockSpec(memory_space=pltpu.SMEM)
PARAMS = pltpu.CompilerParams(vmem_limit_bytes=50 * 1024 * 1024)
BF = jnp.bfloat16


def f32(*shape):
    return jax.ShapeDtypeStruct(shape, jnp.float32)


def b16(*shape):
    return jax.ShapeDtypeStruct(shape, BF)


def split(t):
    high = t.astype(BF)
    return high, (t - high.astype(jnp.float32)).astype(BF)


def dot3(a, b):
    dot = lambda u, v: jnp.dot(u, v, preferred_element_type=jnp.float32)
    return dot(a[0], b[0]) + (dot(a[0], b[1]) + dot(a[1], b[0]))


def permute_kernel(order, *refs):
    half = len(refs) // 2

    def step(j, carry):
        m = order[j]
        for src, dst in zip(refs[:half], refs[half:]):
            dst[j] = src[m]
        return carry

    lax.fori_loop(0, refs[half].shape[0], step, 0, unroll=8)


def send_rows(order, x, columns):
    specs = [pl.BlockSpec((1536, None, 2, 128), lambda i, c=c: (0, c, 0, 0)) for c in columns]
    return pl.pallas_call(
        permute_kernel,
        out_shape=[f32(1536, 2, 128)] * len(columns),
        grid=(1,),
        in_specs=[SMEM] + specs,
        out_specs=[pl.BlockSpec((1536, 2, 128), lambda i: (0, 0, 0))] * len(columns),
        compiler_params=PARAMS,
        name="send_rows",
    )(order, *[x] * len(columns))


def place_rows(order, arrived):
    return pl.pallas_call(
        permute_kernel,
        out_shape=f32(1536, 2, 128),
        in_specs=[SMEM, VMEM],
        out_specs=VMEM,
        compiler_params=PARAMS,
        name="place_rows",
    )(order, arrived)


def pair(ref, index, start, rows):
    left = ref[index + (pl.ds(2 * start, rows, stride=2),)]
    right = ref[index + (pl.ds(2 * start + 1, rows, stride=2),)]
    return jnp.concatenate([left, right], axis=1)


NUMBER = {(0, 1): 0, (0, 2): 1, (0, 3): 2, (1, 2): 3, (1, 3): 4, (2, 3): 5}


def upper_kernel(
    place, lower_fill, upper_fill, own, other, r0, r1, r2, inv, uh, ul, vh, vl, ih, il, corner
):
    here_x, here_y, core, here_col = place[0], place[1], place[2], place[3]
    for half in range(2):
        for i in range(4):
            for k in range(4):
                b = 2 * half + i // 2
                if b == k:
                    continue
                at = (lax.rem(here_x - i + 4, 4), lax.rem(here_y - k + 4, 4))
                rows = slice(128 * (i % 2), 128 * (i % 2) + 128)

                @pl.when(core == half)
                def _():
                    corner[b, k, rows, :] = pair(own, at, 0, 128)

                @pl.when(core != half)
                def _():
                    corner[b, k, rows, :] = pair(other, at, 0, 128)

    for k in range(4):
        ih[k], il[k] = split(inv[k])
    low = {}
    for k in range(4):
        for m in range(k):
            t = corner[k, m]
            for n in range(m):
                e = NUMBER[n, m]
                t = t - dot3(low[k, n], (vh[e], vl[e]))
            keep = (lower_fill[m, k] == 1).astype(jnp.float32)
            low[k, m] = split(dot3(split(t), (ih[m], il[m])) * keep)
        for j in range(k + 1, 4):
            t = corner[k, j]
            for m in range(k):
                e = NUMBER[m, j]
                t = t - dot3(low[k, m], (vh[e], vl[e]))
            keep = (upper_fill[k, j] == 1).astype(jnp.float32)
            vh[NUMBER[k, j]], vl[NUMBER[k, j]] = split(t * keep)
        for c, ref in enumerate((r0, r1, r2)):
            cols = slice(256 * c, 256 * c + 256)
            t = pair(ref, (k,), 0, 256)
            for m in range(k):
                before = slice(256 * m, 256 * m + 256)
                t = t - dot3(low[k, m], (uh[before, cols], ul[before, cols]))
            block = c * 16 + here_col
            keep = ((block > k) & (upper_fill[k, block] == 1)).astype(jnp.float32)
            mine = slice(256 * k, 256 * k + 256)
            uh[mine, cols], ul[mine, cols] = split(t * keep)


def update_kernel(
    place, lower_fill, panels, p0, p1, p2, uh, ul, vh, vl, ih, il, out, lh, ll, kept
):
    here_col, here_row = place[3], place[4]
    i = pl.program_id(0)
    row = lax.broadcasted_iota(jnp.int32, (384, 1), 0)
    blocks = [(3 * i + g) // 2 * 8 + here_row for g in range(3)]
    rowblock = jnp.where(row < 128, blocks[0], jnp.where(row < 256, blocks[1], blocks[2]))
    for k in range(4):
        cols = slice(256 * k, 256 * k + 256)
        t = pair(panels, (0, k), 0, 384)
        for m in range(k):
            e, before = NUMBER[m, k], slice(256 * m, 256 * m + 256)
            t = t - dot3((lh[:, before], ll[:, before]), (vh[e], vl[e]))
        keep = [((b > k) & (lower_fill[k, b] == 1)).astype(jnp.float32) for b in blocks]
        keep = jnp.where(row < 128, keep[0], jnp.where(row < 256, keep[1], keep[2]))
        t = dot3(split(t), (ih[k], il[k])) * keep
        lh[:, cols], ll[:, cols] = split(t)

        @pl.when(here_col == k)
        def _():
            kept[...] = t

    for c, ref in enumerate((p0, p1, p2)):
        cols = slice(256 * c, 256 * c + 256)
        t = dot3((lh[...], ll[...]), (uh[:, cols], ul[:, cols]))
        t = pair(ref, (), 0, 384) - t
        if c == 0:
            t = jnp.where((here_col < 4) & (rowblock > here_col), kept[...], t)
        out[pl.ds(2 * c, 384, stride=6), :] = t[:, :128]
        out[pl.ds(2 * c + 1, 384, stride=6), :] = t[:, 128:]


def whole(*shape):
    return pl.BlockSpec(shape, lambda i: (0,) * len(shape))


def scatter_x(blocks, here_x):
    got = [
        lax.ppermute(blocks[s], "pcol", [(k, k + 4 * s) for k in range(4)]) for s in range(1, 4)
    ]
    return jnp.where(here_x == 0, blocks[0], got[0] + got[1] + got[2])


def spread_z(top, here_z, core):
    def go(value, pairs):
        return lax.ppermute(value, "prow", [(2 * a + c, 2 * b + c) for a, b in pairs for c in (0, 1)])

    away = go(top, [(0, 3), (1, 2)])
    near = go(top, [(0, 1), (1, 0)])
    on = go(away, [(3, 2), (2, 3)])
    d0 = jnp.where(here_z == 0, top, jnp.where(here_z == 1, near, jnp.where(here_z == 2, on, away)))
    d1 = jnp.where(here_z == 1, top, jnp.where(here_z == 0, near, jnp.where(here_z == 3, on, away)))
    mine = jnp.stack([d0, d1])
    other = lax.ppermute(mine, "prow", [(p, p ^ 1) for p in range(8)])
    even, odd = jnp.where(core == 0, mine, other), jnp.where(core == 0, other, mine)
    return jnp.stack([even, odd], axis=1).reshape(4, 512, 128)


def body(matrix, row_order, inverses, lower_fill, upper_fill):
    here_row = lax.axis_index("prow")
    here_col = lax.axis_index("pcol")
    here_x, here_y = here_col // 4, here_col % 4
    here_z, core = here_row // 2, here_row % 2
    x = matrix.reshape(1536, 3, 2, 128)
    targets = row_order.reshape(6, 8, 256)
    local = jnp.arange(1536, dtype=jnp.int32)

    def keys(t):
        owner, row = t // 256 % 8, t // 2048 * 256 + t % 256
        return (owner * 2048 + local) * 2048 + row

    mine = lax.dynamic_slice(targets, (0, here_row, 0), (6, 1, 256)).reshape(1536)
    order = lax.sort(keys(mine)) // 2048 % 2048
    (s0,) = send_rows(order, x, (0,))
    s1, s2 = send_rows(order, x, (1, 2))
    a2a = lambda s: lax.all_to_all(s.reshape(8, 384, 128), "prow", 0, 0, tiled=True)
    g0, g1, g2 = [a2a(s).reshape(1536, 2, 128) for s in (s0, s1, s2)]
    all_keys = lax.sort(keys(targets.transpose(1, 0, 2).reshape(8, 1536)), dimension=1)
    places = lax.dynamic_slice(all_keys, (0, here_row * 192), (8, 192)).reshape(1536) % 2048
    backward = lax.sort(places * 2048 + local) % 2048
    p0, p1, p2 = [place_rows(backward, g).reshape(3072, 128) for g in (g0, g1, g2)]
    quarter = scatter_x(p0.reshape(4, 768, 128), here_x)
    panels = lax.all_gather(quarter, "pcol", axis=0, tiled=True).reshape(4, 4, 768, 128)
    r0, r1, r2 = [spread_z(p[:512], here_z, core) for p in (p0, p1, p2)]
    corner = lax.dynamic_slice(r0, (core * 2, 0, 0), (2, 512, 128)).reshape(4, 256, 128)
    corner = scatter_x(corner, here_x)
    along_y = lambda s: [(q, q // 4 * 4 + (q + s) % 4) for q in range(16)]
    along_x = lambda s: [(q, (q + 4 * s) % 16) for q in range(16)]
    corner = jnp.stack([corner] + [lax.ppermute(corner, "pcol", along_y(s)) for s in (1, 2, 3)])
    corner = jnp.stack([corner] + [lax.ppermute(corner, "pcol", along_x(s)) for s in (1, 2, 3)])
    other = lax.ppermute(corner, "prow", [(p, p ^ 1) for p in range(8)])
    place = jnp.stack([here_x, here_y, core, here_col, here_row]).astype(jnp.int32)
    parts = pl.pallas_call(
        upper_kernel,
        out_shape=[b16(1024, 768)] * 2 + [b16(6, 256, 256)] * 2 + [b16(4, 256, 256)] * 2,
        in_specs=[SMEM] * 3 + [VMEM] * 6,
        out_specs=[VMEM] * 6,
        scratch_shapes=[pltpu.VMEM((4, 4, 256, 256), jnp.float32)],
        compiler_params=PARAMS,
        name="upper",
    )(place, lower_fill, upper_fill, corner, other, r0, r1, r2, inverses)
    rows = pl.BlockSpec((768, 128), lambda i: (i, 0))
    out = pl.pallas_call(
        update_kernel,
        out_shape=f32(9216, 128),
        grid=(4,),
        in_specs=[SMEM, SMEM, pl.BlockSpec((1, 4, 768, 128), lambda i: (i, 0, 0, 0))]
        + [rows] * 3
        + [whole(1024, 768)] * 2
        + [whole(6, 256, 256)] * 2
        + [whole(4, 256, 256)] * 2,
        out_specs=pl.BlockSpec((2304, 128), lambda i: (i, 0)),
        scratch_shapes=[
            pltpu.VMEM((384, 1024), BF),
            pltpu.VMEM((384, 1024), BF),
            pltpu.VMEM((384, 256), jnp.float32),
        ],
        compiler_params=PARAMS,
        name="update",
    )(place, lower_fill, panels, p0, p1, p2, *parts)
    return out.reshape(6, 1, 256, 3, 1, 256)


def solution(mesh):
    in_specs = (P(None, "prow", None, None, "pcol", None), P(), P(), P(), P())
    out_specs = P(None, "prow", None, None, "pcol", None)
    return jax.shard_map(body, mesh=mesh, in_specs=in_specs, out_specs=out_specs, check_vma=False)
```

```python
import jax
import jax.numpy as jnp
from jax import lax
from jax.experimental import pallas as pl
from jax.experimental.pallas import tpu as pltpu
from jax.sharding import PartitionSpec as P

VMEM = pl.BlockSpec(memory_space=pltpu.VMEM)
SMEM = pl.BlockSpec(memory_space=pltpu.SMEM)
PARAMS = pltpu.CompilerParams(vmem_limit_bytes=50 * 1024 * 1024)
BF = jnp.bfloat16


def f32(*shape):
    return jax.ShapeDtypeStruct(shape, jnp.float32)


def b16(*shape):
    return jax.ShapeDtypeStruct(shape, BF)


def split(t):
    high = t.astype(BF)
    return high, (t - high.astype(jnp.float32)).astype(BF)


def dot3(a, b):
    dot = lambda u, v: jnp.dot(u, v, preferred_element_type=jnp.float32)
    return dot(a[0], b[0]) + (dot(a[0], b[1]) + dot(a[1], b[0]))


def first_kernel(targets, x, out, slots, spots, sem):
    @pl.when(pl.program_id(0) == 0)
    def _():
        owner = lax.rem(lax.div(targets[...], 256), 8)
        hot = jnp.concatenate([(owner == d).astype(jnp.float32) for d in range(8)], axis=0)
        r = lax.broadcasted_iota(jnp.int32, (128, 128), 0)
        c = lax.broadcasted_iota(jnp.int32, (128, 128), 1)
        ahead = jnp.dot(hot, (r < c).astype(jnp.float32), preferred_element_type=jnp.float32)
        r = lax.broadcasted_iota(jnp.int32, (96, 96), 0)
        c = lax.broadcasted_iota(jnp.int32, (96, 96), 1)
        earlier = ((c < r) & (lax.div(r, 12) == lax.div(c, 12))).astype(jnp.float32)
        total = jnp.broadcast_to(jnp.sum(hot, axis=1, keepdims=True), (96, 128))
        ahead = ahead + jnp.dot(earlier, total, preferred_element_type=jnp.float32)
        slot = jnp.zeros((12, 128), jnp.float32)
        for d in range(8):
            part = slice(12 * d, 12 * d + 12)
            slot = slot + hot[part] * (ahead[part] + 192.0 * d)
        slots[...] = slot.astype(jnp.int32)
        copy = pltpu.make_async_copy(slots, spots, sem)
        copy.start()
        copy.wait()

    base = pl.program_id(0) * 3

    def step(j, carry):
        for q in range(3):
            out[spots[base + q, j]] = x[384 * q + 3 * j]
        return carry

    lax.fori_loop(0, 128, step, 0, unroll=4)


def send_first(targets, x):
    return pl.pallas_call(
        first_kernel,
        out_shape=(f32(1536, 2, 128), jax.ShapeDtypeStruct((12, 128), jnp.int32)),
        grid=(4,),
        in_specs=[
            pl.BlockSpec((12, 128), lambda i: (0, 0)),
            pl.BlockSpec((1152, 2, 128), lambda i: (i, 0, 0)),
        ],
        out_specs=(
            pl.BlockSpec((1536, 2, 128), lambda i: (0, 0, 0)),
            pl.BlockSpec((12, 128), lambda i: (0, 0)),
        ),
        scratch_shapes=[pltpu.SMEM((12, 128), jnp.int32), pltpu.SemaphoreType.DMA],
        compiler_params=PARAMS,
        name="send_first",
    )(targets, x)


def rest_kernel(slots, x, second, third):
    base = pl.program_id(0) * 3

    def step(j, carry):
        for q in range(3):
            d, r = slots[base + q, j], 384 * q + 3 * j
            second[d] = x[r + 1]
            third[d] = x[r + 2]
        return carry

    lax.fori_loop(0, 128, step, 0, unroll=4)


def send_rest(slots, x):
    return pl.pallas_call(
        rest_kernel,
        out_shape=[f32(1536, 2, 128)] * 2,
        grid=(4,),
        in_specs=[SMEM, pl.BlockSpec((1152, 2, 128), lambda i: (i, 0, 0))],
        out_specs=[pl.BlockSpec((1536, 2, 128), lambda i: (0, 0, 0))] * 2,
        compiler_params=PARAMS,
        name="send_rest",
    )(slots, x)


def top_kernel(order, p0, p1, arrived, out):
    out[:256] = p0[...]
    out[256:512] = p1[...]

    def step(d, carry):
        out[512 + d] = arrived[order[d]]
        return carry

    lax.fori_loop(0, 256, step, 0, unroll=8)


def top_rows(order, p0, p1, arrived):
    own = pl.BlockSpec((256, 2, 128), lambda i: (0, 0, 0))
    return pl.pallas_call(
        top_kernel,
        out_shape=f32(768, 2, 128),
        grid=(1,),
        in_specs=[SMEM, own, own, pl.BlockSpec((1536, 2, 128), lambda i: (0, 0, 0))],
        out_specs=pl.BlockSpec((768, 2, 128), lambda i: (0, 0, 0)),
        compiler_params=PARAMS,
        name="top_rows",
    )(order, p0, p1, arrived)


def place_kernel(order, arrived, out):
    def step(d, carry):
        out[d] = arrived[order[d]]
        return carry

    lax.fori_loop(0, 1536, step, 0, unroll=8)


def place_rows(order, arrived):
    return pl.pallas_call(
        place_kernel,
        out_shape=f32(*arrived.shape),
        in_specs=[SMEM, VMEM],
        out_specs=VMEM,
        compiler_params=PARAMS,
        name="place_rows",
    )(order, arrived)


def corner_rows_kernel(place, pieces, out):
    here_y, here_row = place[1], place[4]
    for j in range(3):
        k = j + (here_row <= j).astype(jnp.int32)
        out[j] = pieces[lax.rem(here_y - k + 4, 4)]


def pair(ref, index, rows, first=0):
    left = ref[index + (pl.ds(first, rows, stride=2),)]
    right = ref[index + (pl.ds(first + 1, rows, stride=2),)]
    return jnp.concatenate([left, right], axis=1)


def block(k):
    return slice(256 * k, 256 * k + 256)


RIGHT = (0, 768, 1280, 1536)
LEFT = (0, 0, 256, 768)


def right(k, j):
    return block(RIGHT[k] // 256 + j - k - 1)


def left(k, m):
    return block(LEFT[k] // 256 + m)


def corner_kernel(place, lower_fill, upper_fill, mine, other, inv, vh, vl, ih, il, wh, wl):
    here_x, core = place[0], place[2]

    def corner(b, k):
        parts = []
        for i in range(4):
            at = (lax.rem(here_x - i + 4, 4), b // 2, k - (k > b))
            parts.append(jnp.where(core == b % 2, pair(mine, at, 64), pair(other, at, 64)))
        return jnp.concatenate(parts, axis=0)

    for k in range(4):
        ih[k], il[k] = split(inv[k])
    low, high = {}, {}
    for k in range(4):
        for m in range(k):
            t = dot3(split(corner(k, m)), (ih[m], il[m]))
            for n in range(m):
                t = t - dot3(low[k, n], (vh[:, right(n, m)], vl[:, right(n, m)]))
            keep = (lower_fill[m, k] == 1).astype(jnp.float32)
            low[k, m] = split(t * keep)
            wh[:, left(k, m)], wl[:, left(k, m)] = low[k, m]
        for j in range(k + 1, 4):
            t = corner(k, j)
            for m in range(k):
                t = t - dot3(low[k, m], high[m, j])
            keep = (upper_fill[k, j] == 1).astype(jnp.float32)
            high[k, j] = split(t * keep)
            t = dot3(high[k, j], (ih[j], il[j]))
            vh[:, right(k, j)], vl[:, right(k, j)] = split(t)


def update_kernel(
    place, lower_fill, upper_fill, panels, p0, p1, p2, mine, other, vh, vl, ih, il, wh, wl,
    out, acc, lh, ll, uh, ul
):
    core, here_col, here_row = place[2], place[3], place[4]

    @pl.when(pl.program_id(0) == 0)
    def _():
        for k in range(4):
            before = slice(0, 256 * k)
            lefts = slice(LEFT[k], LEFT[k] + 256 * k)
            for c in range(3):
                at, first = (k // 2,), 512 * c
                t = jnp.where(
                    core == k % 2, pair(mine, at, 256, first), pair(other, at, 256, first)
                )
                if k:
                    t = t - dot3(
                        (wh[:, lefts], wl[:, lefts]), (uh[before, block(c)], ul[before, block(c)])
                    )
                j = c * 16 + here_col
                keep = ((j > k) & (upper_fill[k, j] == 1)).astype(jnp.float32)
                uh[block(k), block(c)], ul[block(k), block(c)] = split(t * keep)

    group = lax.broadcasted_iota(jnp.int32, (384, 1), 0) // 64

    def per_row(values):
        t = values[5]
        for g in range(5):
            t = jnp.where(group == g, values[g], t)
        return t

    blocks = [g * 8 + here_row for g in range(6)]
    for k in range(4):
        acc[:, block(k)] = dot3(split(pair(panels, (0, k), 384)), (ih[k], il[k]))
    for k in range(4):
        keep = [((b > k) & (lower_fill[k, b] == 1)).astype(jnp.float32) for b in blocks]
        t = acc[:, block(k)] * per_row(keep)
        acc[:, block(k)] = t
        high, low = split(t)
        lh[:, block(k)], ll[:, block(k)] = high, low
        if k < 3:
            after = slice(256 * k + 256, 1024)
            rights = slice(RIGHT[k], RIGHT[k + 1])
            acc[:, after] -= dot3((high, low), (vh[:, rights], vl[:, rights]))
    done = (here_col < 4) & (per_row(blocks) > here_col)
    own = pl.ds(pl.multiple_of(jnp.minimum(here_col, 3) * 256, 256), 256)
    for c in range(3):
        t = dot3((lh[...], ll[...]), (uh[:, block(c)], ul[:, block(c)]))
        for g in range(6):
            here = slice(64 * g, 64 * g + 64)
            new = pair((p0, p1, p2)[c], (g, 0), 64) - t[here]
            if c == 0:
                new = jnp.where(done[here], acc[here, own], new)
            out[g, 0, pl.ds(2 * c, 64, stride=6), :] = new[:, :128]
            out[g, 0, pl.ds(2 * c + 1, 64, stride=6), :] = new[:, 128:]


def whole(*shape):
    return pl.BlockSpec(shape, lambda i: (0,) * len(shape))


def scatter_x(blocks):
    return [
        lax.ppermute(blocks[s], "pcol", [(k, k + 4 * s) for k in range(4)]) for s in range(1, 4)
    ]


def scattered(block, got, here_x):
    return jnp.where(here_x == 0, block, got[0] + got[1] + got[2])


def hop_z(value, pairs):
    return lax.ppermute(value, "prow", [(2 * a + c, 2 * b + c) for a, b in pairs for c in (0, 1)])


def spread_z(top, hops, here_z):
    away, near = hops
    on = hop_z(away, [(3, 2), (2, 3)])
    d0 = jnp.where(here_z == 0, top, jnp.where(here_z == 1, near, jnp.where(here_z == 2, on, away)))
    d1 = jnp.where(here_z == 1, top, jnp.where(here_z == 0, near, jnp.where(here_z == 3, on, away)))
    return jnp.stack([d0, d1])


def with_other(mine):
    return mine, lax.ppermute(mine, "prow", [(p, p ^ 1) for p in range(8)])


def first_hops(top):
    return hop_z(top, [(0, 3), (1, 2)]), hop_z(top, [(0, 1), (1, 0)])


def body(matrix, row_order, inverses, lower_fill, upper_fill):
    here_row = lax.axis_index("prow")
    here_col = lax.axis_index("pcol")
    here_x, here_y = here_col // 4, here_col % 4
    here_z, core = here_row // 2, here_row % 2
    x = matrix.reshape(4608, 2, 128)
    targets = row_order.reshape(6, 8, 256)
    local = jnp.arange(1536, dtype=jnp.int32)

    def keys(t):
        owner, row = t // 256 % 8, t // 2048 * 256 + t % 256
        return (owner * 2048 + local) * 2048 + row

    mine = lax.dynamic_slice(targets, (0, here_row, 0), (6, 1, 256)).reshape(12, 128)
    s0, slots = send_first(mine, x)
    s1, s2 = send_rest(slots, x)
    a2a = lambda s: lax.all_to_all(s.reshape(8, -1, 128), "prow", 0, 0, tiled=True)
    g0 = a2a(s0).reshape(1536, 2, 128)
    all_keys = lax.sort(keys(targets.transpose(1, 0, 2).reshape(8, 1536)), dimension=1)
    places = lax.dynamic_slice(all_keys, (0, here_row * 192), (8, 192)).reshape(1536) % 2048
    backward = lax.sort(places * 2048 + local) % 2048
    backward, s1 = lax.optimization_barrier((backward, s1))
    g1, g2 = [a2a(s).reshape(1536, 2, 128) for s in (s1, s2)]
    p0 = place_rows(backward, g0)
    parts0 = p0.reshape(6, 4, 128, 128)
    got, g1 = lax.optimization_barrier((scatter_x([parts0[:, i] for i in range(4)]), g1))
    quarter = scattered(parts0[:, 0], got, here_x)
    panels = lax.all_gather(quarter.reshape(768, 128), "pcol", axis=0, tiled=True)
    panels = panels.reshape(4, 4, 768, 128)
    p1 = place_rows(backward, g1)
    along_y = lambda s: [(q, q // 4 * 4 + (q + s) % 4) for q in range(16)]
    along_x = lambda s: [(q, (q + 4 * s) % 16) for q in range(16)]
    shifts = lambda v, along: [lax.ppermute(v, "pcol", along(s)) for s in (1, 2, 3)]
    corner, p1 = lax.optimization_barrier((jnp.stack([quarter[0]] + shifts(quarter[0], along_y)), p1))
    place = jnp.stack([here_x, here_y, core, here_col, here_row]).astype(jnp.int32)
    corner = pl.pallas_call(
        corner_rows_kernel,
        out_shape=f32(3, 128, 128),
        in_specs=[SMEM, VMEM],
        out_specs=VMEM,
        compiler_params=PARAMS,
        name="corner_rows",
    )(place, corner)
    hops, g2 = lax.optimization_barrier((first_hops(corner), g2))
    corner = spread_z(corner, hops, here_z)
    top = top_rows(backward[:256], p0, p1, g2).reshape(1536, 128)
    far, hops = lax.optimization_barrier((shifts(corner, along_x), first_hops(top)))
    corner = with_other(jnp.stack([corner] + far))
    p2 = place_rows(backward, g2)
    rows = with_other(spread_z(top, hops, here_z))
    parts = pl.pallas_call(
        corner_kernel,
        out_shape=[b16(256, 1536)] * 2 + [b16(4, 256, 256)] * 2 + [b16(256, 1536)] * 2,
        in_specs=[SMEM] * 3 + [VMEM] * 3,
        out_specs=[VMEM] * 6,
        compiler_params=PARAMS,
        name="corner",
    )(place, lower_fill, upper_fill, *corner, inverses)
    part = lambda n: pl.BlockSpec((6, 1, n, 128), lambda i: (0, i, 0, 0))
    out = pl.pallas_call(
        update_kernel,
        out_shape=f32(6, 4, 384, 128),
        grid=(4,),
        in_specs=[SMEM] * 3
        + [pl.BlockSpec((1, 4, 768, 128), lambda i: (i, 0, 0, 0))]
        + [part(128)] * 3
        + [whole(2, 1536, 128)] * 2
        + [whole(256, 1536)] * 2
        + [whole(4, 256, 256)] * 2
        + [whole(256, 1536)] * 2,
        out_specs=part(384),
        scratch_shapes=[
            pltpu.VMEM((384, 1024), jnp.float32),
            pltpu.VMEM((384, 1024), BF),
            pltpu.VMEM((384, 1024), BF),
            pltpu.VMEM((1024, 768), BF),
            pltpu.VMEM((1024, 768), BF),
        ],
        compiler_params=PARAMS,
        name="update",
    )(
        place, lower_fill, upper_fill, panels,
        *[p.reshape(6, 4, 128, 128) for p in (p0, p1, p2)], *rows, *parts
    )
    return out.reshape(6, 1, 256, 3, 1, 256)


def solution(mesh):
    in_specs = (P(None, "prow", None, None, "pcol", None), P(), P(), P(), P())
    out_specs = P(None, "prow", None, None, "pcol", None)
    return jax.shard_map(body, mesh=mesh, in_specs=in_specs, out_specs=out_specs, check_vma=False)
```

```python
import jax
import jax.numpy as jnp
from jax import lax
from jax.experimental import pallas as pl
from jax.experimental.pallas import tpu as pltpu
from jax.sharding import PartitionSpec as P

VMEM = pl.BlockSpec(memory_space=pltpu.VMEM)
SMEM = pl.BlockSpec(memory_space=pltpu.SMEM)
PARAMS = pltpu.CompilerParams(vmem_limit_bytes=14 * 1024 * 1024)
LARGE = pltpu.CompilerParams(vmem_limit_bytes=40 * 1024 * 1024)
BF = jnp.bfloat16


def f32(*shape):
    return jax.ShapeDtypeStruct(shape, jnp.float32)


def b16(*shape):
    return jax.ShapeDtypeStruct(shape, BF)


def split(t):
    high = t.astype(BF)
    return high, (t - high.astype(jnp.float32)).astype(BF)


def dot3(a, b):
    dot = lambda u, v: jnp.dot(u, v, preferred_element_type=jnp.float32)
    return dot(a[0], b[0]) + (dot(a[0], b[1]) + dot(a[1], b[0]))


def first_kernel(targets, x, out, slots, spots, sem):
    @pl.when(pl.program_id(0) == 0)
    def _():
        owner = lax.rem(lax.div(targets[...], 256), 8)
        hot = jnp.concatenate([(owner == d).astype(jnp.float32) for d in range(8)], axis=0)
        r = lax.broadcasted_iota(jnp.int32, (128, 128), 0)
        c = lax.broadcasted_iota(jnp.int32, (128, 128), 1)
        ahead = jnp.dot(hot, (r < c).astype(jnp.float32), preferred_element_type=jnp.float32)
        r = lax.broadcasted_iota(jnp.int32, (96, 96), 0)
        c = lax.broadcasted_iota(jnp.int32, (96, 96), 1)
        earlier = ((c < r) & (lax.div(r, 12) == lax.div(c, 12))).astype(jnp.float32)
        total = jnp.broadcast_to(jnp.sum(hot, axis=1, keepdims=True), (96, 128))
        ahead = ahead + jnp.dot(earlier, total, preferred_element_type=jnp.float32)
        slot = jnp.zeros((12, 128), jnp.float32)
        for d in range(8):
            part = slice(12 * d, 12 * d + 12)
            slot = slot + hot[part] * (ahead[part] + 192.0 * d)
        slots[...] = slot.astype(jnp.int32)
        copy = pltpu.make_async_copy(slots, spots, sem)
        copy.start()
        copy.wait()

    base = pl.program_id(0) * 3

    def step(j, carry):
        for q in range(3):
            out[spots[base + q, j]] = x[384 * q + 3 * j]
        return carry

    lax.fori_loop(0, 128, step, 0, unroll=4)


def send_first(targets, x):
    return pl.pallas_call(
        first_kernel,
        out_shape=(f32(1536, 2, 128), jax.ShapeDtypeStruct((12, 128), jnp.int32)),
        grid=(4,),
        in_specs=[
            pl.BlockSpec((12, 128), lambda i: (0, 0)),
            pl.BlockSpec((1152, 2, 128), lambda i: (i, 0, 0)),
        ],
        out_specs=(
            pl.BlockSpec((1536, 2, 128), lambda i: (0, 0, 0)),
            pl.BlockSpec((12, 128), lambda i: (0, 0)),
        ),
        scratch_shapes=[pltpu.SMEM((12, 128), jnp.int32), pltpu.SemaphoreType.DMA],
        compiler_params=PARAMS,
        name="send_first",
    )(targets, x)


def rest_kernel(slots, x, second, third):
    base = pl.program_id(0) * 3

    def step(j, carry):
        for q in range(3):
            d, r = slots[base + q, j], 384 * q + 3 * j
            second[d] = x[r + 1]
            third[d] = x[r + 2]
        return carry

    lax.fori_loop(0, 128, step, 0, unroll=4)


def send_rest(slots, x):
    return pl.pallas_call(
        rest_kernel,
        out_shape=[f32(1536, 2, 128)] * 2,
        grid=(4,),
        in_specs=[SMEM, pl.BlockSpec((1152, 2, 128), lambda i: (i, 0, 0))],
        out_specs=[pl.BlockSpec((1536, 2, 128), lambda i: (0, 0, 0))] * 2,
        compiler_params=PARAMS,
        name="send_rest",
    )(slots, x)


def top_kernel(order, p0, p1, arrived, out):
    out[:256] = p0[...]
    out[256:512] = p1[...]

    def step(d, carry):
        out[512 + d] = arrived[order[d]]
        return carry

    lax.fori_loop(0, 256, step, 0, unroll=8)


def top_rows(order, p0, p1, arrived):
    own = pl.BlockSpec((256, 2, 128), lambda i: (0, 0, 0))
    return pl.pallas_call(
        top_kernel,
        out_shape=f32(768, 2, 128),
        grid=(1,),
        in_specs=[SMEM, own, own, pl.BlockSpec((1536, 2, 128), lambda i: (0, 0, 0))],
        out_specs=pl.BlockSpec((768, 2, 128), lambda i: (0, 0, 0)),
        compiler_params=PARAMS,
        name="top_rows",
    )(order, p0, p1, arrived)


def place_kernel(order, arrived, out):
    def step(d, carry):
        out[d] = arrived[order[d]]
        return carry

    lax.fori_loop(0, 1536, step, 0, unroll=8)


def place_rows(order, arrived):
    return pl.pallas_call(
        place_kernel,
        out_shape=f32(*arrived.shape),
        in_specs=[SMEM, VMEM],
        out_specs=VMEM,
        compiler_params=PARAMS,
        name="place_rows",
    )(order, arrived)


def corner_rows_kernel(place, pieces, out):
    here_y, here_row = place[1], place[4]
    for j in range(3):
        k = j + (here_row <= j).astype(jnp.int32)
        out[j] = pieces[lax.rem(here_y - k + 4, 4)]


def pair(ref, index, rows, first=0):
    left = ref[index + (pl.ds(first, rows, stride=2),)]
    right = ref[index + (pl.ds(first + 1, rows, stride=2),)]
    return jnp.concatenate([left, right], axis=1)


def block(k):
    return slice(256 * k, 256 * k + 256)


RIGHT = (0, 768, 1280, 1536)
LEFT = (0, 0, 256, 768)


def right(k, j):
    return block(RIGHT[k] // 256 + j - k - 1)


def left(k, m):
    return block(LEFT[k] // 256 + m)


def corner_factors(place, lower_fill, upper_fill, mine, other, inv, vh, vl, wh, wl, ih, il):
    here_x, core = place[0], place[2]

    def corner(b, k):
        parts = []
        for i in range(4):
            at = (lax.rem(here_x - i + 4, 4), b // 2, k - (k > b))
            parts.append(jnp.where(core == b % 2, pair(mine, at, 64), pair(other, at, 64)))
        return jnp.concatenate(parts, axis=0)

    for k in range(4):
        ih[k], il[k] = split(inv[k])
    low, high = {}, {}
    for k in range(4):
        for m in range(k):
            t = dot3(split(corner(k, m)), (ih[m], il[m]))
            for n in range(m):
                t = t - dot3(low[k, n], (vh[:, right(n, m)], vl[:, right(n, m)]))
            keep = (lower_fill[m, k] == 1).astype(jnp.float32)
            low[k, m] = split(t * keep)
            wh[:, left(k, m)], wl[:, left(k, m)] = low[k, m]
        for j in range(k + 1, 4):
            t = corner(k, j)
            for m in range(k):
                t = t - dot3(low[k, m], high[m, j])
            keep = (upper_fill[k, j] == 1).astype(jnp.float32)
            high[k, j] = split(t * keep)
            t = dot3(high[k, j], (ih[j], il[j]))
            vh[:, right(k, j)], vl[:, right(k, j)] = split(t)


def scale_kernel(panels, inv, out):
    for k in range(4):
        out[:, block(k)] = dot3(split(pair(panels, (0, k), 384)), split(inv[k]))


def update_kernel(
    place, lower_fill, upper_fill, scaled, p0, p1, p2, mine, other, mine_c, other_c, inv,
    out, acc, lh, ll, uh, ul, vh, vl, wh, wl, ih, il
):
    core, here_col, here_row = place[2], place[3], place[4]

    @pl.when(pl.program_id(0) == 0)
    def _():
        corner_factors(
            place, lower_fill, upper_fill, mine_c, other_c, inv, vh, vl, wh, wl, ih, il
        )
        for k in range(4):
            before = slice(0, 256 * k)
            lefts = slice(LEFT[k], LEFT[k] + 256 * k)
            for c in range(3):
                at, first = (k // 2,), 512 * c
                t = jnp.where(
                    core == k % 2, pair(mine, at, 256, first), pair(other, at, 256, first)
                )
                if k:
                    t = t - dot3(
                        (wh[:, lefts], wl[:, lefts]), (uh[before, block(c)], ul[before, block(c)])
                    )
                j = c * 16 + here_col
                keep = ((j > k) & (upper_fill[k, j] == 1)).astype(jnp.float32)
                uh[block(k), block(c)], ul[block(k), block(c)] = split(t * keep)

    group = lax.broadcasted_iota(jnp.int32, (384, 1), 0) // 64

    def per_row(values):
        t = values[5]
        for g in range(5):
            t = jnp.where(group == g, values[g], t)
        return t

    blocks = [g * 8 + here_row for g in range(6)]
    for k in range(4):
        keep = [((b > k) & (lower_fill[k, b] == 1)).astype(jnp.float32) for b in blocks]
        t = (acc if k else scaled)[:, block(k)] * per_row(keep)
        acc[:, block(k)] = t
        high, low = split(t)
        lh[:, block(k)], ll[:, block(k)] = high, low
        if k < 3:
            after = slice(256 * k + 256, 1024)
            rights = slice(RIGHT[k], RIGHT[k + 1])
            t = dot3((high, low), (vh[:, rights], vl[:, rights]))
            acc[:, after] = (acc if k else scaled)[:, after] - t
    done = (here_col < 4) & (per_row(blocks) > here_col)
    own = pl.ds(pl.multiple_of(jnp.minimum(here_col, 3) * 256, 256), 256)
    for c in range(3):
        t = dot3((lh[...], ll[...]), (uh[:, block(c)], ul[:, block(c)]))
        for g in range(6):
            here = slice(64 * g, 64 * g + 64)
            new = pair((p0, p1, p2)[c], (g, 0), 64) - t[here]
            if c == 0:
                new = jnp.where(done[here], acc[here, own], new)
            out[g, 0, pl.ds(2 * c, 64, stride=6), :] = new[:, :128]
            out[g, 0, pl.ds(2 * c + 1, 64, stride=6), :] = new[:, 128:]


def whole(*shape):
    return pl.BlockSpec(shape, lambda i: (0,) * len(shape))


def scatter_x(blocks):
    return [
        lax.ppermute(blocks[s], "pcol", [(k, k + 4 * s) for k in range(4)]) for s in range(1, 4)
    ]


def scattered(block, got, here_x):
    return jnp.where(here_x == 0, block, got[0] + got[1] + got[2])


def hop_z(value, pairs):
    return lax.ppermute(value, "prow", [(2 * a + c, 2 * b + c) for a, b in pairs for c in (0, 1)])


def spread_z(top, hops, here_z):
    away, near = hops
    on = hop_z(away, [(3, 2), (2, 3)])
    d0 = jnp.where(here_z == 0, top, jnp.where(here_z == 1, near, jnp.where(here_z == 2, on, away)))
    d1 = jnp.where(here_z == 1, top, jnp.where(here_z == 0, near, jnp.where(here_z == 3, on, away)))
    return jnp.stack([d0, d1])


def with_other(mine):
    return mine, lax.ppermute(mine, "prow", [(p, p ^ 1) for p in range(8)])


def first_hops(top):
    return hop_z(top, [(0, 3), (1, 2)]), hop_z(top, [(0, 1), (1, 0)])


def body(matrix, row_order, inverses, lower_fill, upper_fill):
    here_row = lax.axis_index("prow")
    here_col = lax.axis_index("pcol")
    here_x, here_y = here_col // 4, here_col % 4
    here_z, core = here_row // 2, here_row % 2
    x = matrix.reshape(4608, 2, 128)
    targets = row_order.reshape(6, 8, 256)
    local = jnp.arange(1536, dtype=jnp.int32)

    def keys(t):
        owner, row = t // 256 % 8, t // 2048 * 256 + t % 256
        return (owner * 2048 + local) * 2048 + row

    mine = lax.dynamic_slice(targets, (0, here_row, 0), (6, 1, 256)).reshape(12, 128)
    s0, slots = send_first(mine, x)
    s1, s2 = send_rest(slots, x)
    a2a = lambda s: lax.all_to_all(s.reshape(8, -1, 128), "prow", 0, 0, tiled=True)
    g0 = a2a(s0).reshape(1536, 2, 128)
    all_keys = lax.sort(keys(targets.transpose(1, 0, 2).reshape(8, 1536)), dimension=1)
    places = lax.dynamic_slice(all_keys, (0, here_row * 192), (8, 192)).reshape(1536) % 2048
    backward = lax.sort(places * 2048 + local) % 2048
    p0 = place_rows(backward, g0)
    p0, s1 = lax.optimization_barrier((p0, s1))
    g1, g2 = [a2a(s).reshape(1536, 2, 128) for s in (s1, s2)]
    parts0 = p0.reshape(6, 4, 128, 128)
    got, g1 = lax.optimization_barrier((scatter_x([parts0[:, i] for i in range(4)]), g1))
    quarter = scattered(parts0[:, 0], got, here_x)
    panels = lax.all_gather(quarter.reshape(768, 128), "pcol", axis=0, tiled=True)
    panels = panels.reshape(4, 4, 768, 128)
    p1 = place_rows(backward, g1)
    along_y = lambda s: [(q, q // 4 * 4 + (q + s) % 4) for q in range(16)]
    along_x = lambda s: [(q, (q + 4 * s) % 16) for q in range(16)]
    shifts = lambda v, along: [lax.ppermute(v, "pcol", along(s)) for s in (1, 2, 3)]
    corner, p1 = lax.optimization_barrier((jnp.stack([quarter[0]] + shifts(quarter[0], along_y)), p1))
    place = jnp.stack([here_x, here_y, core, here_col, here_row]).astype(jnp.int32)
    corner = pl.pallas_call(
        corner_rows_kernel,
        out_shape=f32(3, 128, 128),
        in_specs=[SMEM, VMEM],
        out_specs=VMEM,
        compiler_params=PARAMS,
        name="corner_rows",
    )(place, corner)
    hops, g2 = lax.optimization_barrier((first_hops(corner), g2))
    corner = spread_z(corner, hops, here_z)
    top = top_rows(backward[:256], p0, p1, g2).reshape(1536, 128)
    corner, top = lax.optimization_barrier((corner, top))
    rows = with_other(spread_z(top, first_hops(top), here_z))
    p2 = place_rows(backward, g2)
    corner, panels, p2 = lax.optimization_barrier((corner, panels, p2))
    scaled = pl.pallas_call(
        scale_kernel,
        out_shape=f32(1536, 1024),
        grid=(4,),
        in_specs=[pl.BlockSpec((1, 4, 768, 128), lambda i: (i, 0, 0, 0)), whole(4, 256, 256)],
        out_specs=pl.BlockSpec((384, 1024), lambda i: (i, 0)),
        compiler_params=PARAMS,
        name="scale",
    )(panels, inverses)
    far, scaled = lax.optimization_barrier((shifts(corner, along_x), scaled))
    corner = with_other(jnp.stack([corner] + far))
    part = lambda n: pl.BlockSpec((6, 1, n, 128), lambda i: (0, i, 0, 0))
    out = pl.pallas_call(
        update_kernel,
        out_shape=f32(6, 4, 384, 128),
        grid=(4,),
        in_specs=[SMEM] * 3
        + [pl.BlockSpec((384, 1024), lambda i: (i, 0))]
        + [part(128)] * 3
        + [whole(2, 1536, 128)] * 2
        + [whole(4, 2, 3, 128, 128)] * 2
        + [whole(4, 256, 256)],
        out_specs=part(384),
        scratch_shapes=[
            pltpu.VMEM((384, 1024), jnp.float32),
            pltpu.VMEM((384, 1024), BF),
            pltpu.VMEM((384, 1024), BF),
        ]
        + [pltpu.VMEM((1024, 768), BF)] * 2
        + [pltpu.VMEM((256, 1536), BF)] * 4
        + [pltpu.VMEM((4, 256, 256), BF)] * 2,
        compiler_params=LARGE,
        name="update",
    )(
        place, lower_fill, upper_fill, scaled,
        *[p.reshape(6, 4, 128, 128) for p in (p0, p1, p2)], *rows, *corner, inverses
    )
    return out.reshape(6, 1, 256, 3, 1, 256)


def solution(mesh):
    in_specs = (P(None, "prow", None, None, "pcol", None), P(), P(), P(), P())
    out_specs = P(None, "prow", None, None, "pcol", None)
    return jax.shard_map(body, mesh=mesh, in_specs=in_specs, out_specs=out_specs, check_vma=False)
```

```python
import jax
import jax.numpy as jnp
from jax import lax
from jax.experimental import pallas as pl
from jax.experimental.pallas import tpu as pltpu
from jax.sharding import PartitionSpec as P

VMEM = pl.BlockSpec(memory_space=pltpu.VMEM)
SMEM = pl.BlockSpec(memory_space=pltpu.SMEM)
PARAMS = pltpu.CompilerParams(vmem_limit_bytes=14 * 1024 * 1024)
LARGE = pltpu.CompilerParams(vmem_limit_bytes=40 * 1024 * 1024)
BF = jnp.bfloat16


def f32(*shape):
    return jax.ShapeDtypeStruct(shape, jnp.float32)


def b16(*shape):
    return jax.ShapeDtypeStruct(shape, BF)


def split(t):
    high = t.astype(BF)
    return high, (t - high.astype(jnp.float32)).astype(BF)


def dot3(a, b):
    dot = lambda u, v: jnp.dot(u, v, preferred_element_type=jnp.float32)
    return dot(a[0], b[0]) + (dot(a[0], b[1]) + dot(a[1], b[0]))


def first_kernel(targets, x, out, slots, spots, sem):
    @pl.when(pl.program_id(0) == 0)
    def _():
        owner = lax.rem(lax.div(targets[...], 256), 8)
        hot = jnp.concatenate([(owner == d).astype(jnp.float32) for d in range(8)], axis=0)
        r = lax.broadcasted_iota(jnp.int32, (128, 128), 0)
        c = lax.broadcasted_iota(jnp.int32, (128, 128), 1)
        ahead = jnp.dot(hot, (r < c).astype(jnp.float32), preferred_element_type=jnp.float32)
        r = lax.broadcasted_iota(jnp.int32, (96, 96), 0)
        c = lax.broadcasted_iota(jnp.int32, (96, 96), 1)
        earlier = ((c < r) & (lax.div(r, 12) == lax.div(c, 12))).astype(jnp.float32)
        total = jnp.broadcast_to(jnp.sum(hot, axis=1, keepdims=True), (96, 128))
        ahead = ahead + jnp.dot(earlier, total, preferred_element_type=jnp.float32)
        slot = jnp.zeros((12, 128), jnp.float32)
        for d in range(8):
            part = slice(12 * d, 12 * d + 12)
            slot = slot + hot[part] * (ahead[part] + 192.0 * d)
        slots[...] = slot.astype(jnp.int32)
        copy = pltpu.make_async_copy(slots, spots, sem)
        copy.start()
        copy.wait()

    base = pl.program_id(0) * 3

    def step(j, carry):
        for q in range(3):
            out[spots[base + q, j]] = x[384 * q + 3 * j]
        return carry

    lax.fori_loop(0, 128, step, 0, unroll=4)


def send_first(targets, x):
    return pl.pallas_call(
        first_kernel,
        out_shape=(f32(1536, 2, 128), jax.ShapeDtypeStruct((12, 128), jnp.int32)),
        grid=(4,),
        in_specs=[
            pl.BlockSpec((12, 128), lambda i: (0, 0)),
            pl.BlockSpec((1152, 2, 128), lambda i: (i, 0, 0)),
        ],
        out_specs=(
            pl.BlockSpec((1536, 2, 128), lambda i: (0, 0, 0)),
            pl.BlockSpec((12, 128), lambda i: (0, 0)),
        ),
        scratch_shapes=[pltpu.SMEM((12, 128), jnp.int32), pltpu.SemaphoreType.DMA],
        compiler_params=PARAMS,
        name="send_first",
    )(targets, x)


def rest_kernel(slots, x, second, third):
    base = pl.program_id(0) * 3

    def step(j, carry):
        for q in range(3):
            d, r = slots[base + q, j], 384 * q + 3 * j
            second[d] = x[r + 1]
            third[d] = x[r + 2]
        return carry

    lax.fori_loop(0, 128, step, 0, unroll=4)


def send_rest(slots, x):
    return pl.pallas_call(
        rest_kernel,
        out_shape=[f32(1536, 2, 128)] * 2,
        grid=(4,),
        in_specs=[SMEM, pl.BlockSpec((1152, 2, 128), lambda i: (i, 0, 0))],
        out_specs=[pl.BlockSpec((1536, 2, 128), lambda i: (0, 0, 0))] * 2,
        compiler_params=PARAMS,
        name="send_rest",
    )(slots, x)


def top_kernel(order, p0, p1, arrived, out):
    out[:256] = p0[...]
    out[256:512] = p1[...]

    def step(d, carry):
        out[512 + d] = arrived[order[d]]
        return carry

    lax.fori_loop(0, 256, step, 0, unroll=8)


def top_rows(order, p0, p1, arrived):
    own = pl.BlockSpec((256, 2, 128), lambda i: (0, 0, 0))
    return pl.pallas_call(
        top_kernel,
        out_shape=f32(768, 2, 128),
        grid=(1,),
        in_specs=[SMEM, own, own, pl.BlockSpec((1536, 2, 128), lambda i: (0, 0, 0))],
        out_specs=pl.BlockSpec((768, 2, 128), lambda i: (0, 0, 0)),
        compiler_params=PARAMS,
        name="top_rows",
    )(order, p0, p1, arrived)


def place_kernel(order, arrived, out):
    def step(d, carry):
        out[d] = arrived[order[d]]
        return carry

    lax.fori_loop(0, 1536, step, 0, unroll=8)


def place_rows(order, arrived):
    return pl.pallas_call(
        place_kernel,
        out_shape=f32(*arrived.shape),
        in_specs=[SMEM, VMEM],
        out_specs=VMEM,
        compiler_params=PARAMS,
        name="place_rows",
    )(order, arrived)


def corner_rows_kernel(place, pieces, out):
    here_y, here_row = place[1], place[4]
    for j in range(3):
        k = j + (here_row <= j).astype(jnp.int32)
        out[j] = pieces[lax.rem(here_y - k + 4, 4)]


def pair(ref, index, rows, first=0):
    left = ref[index + (pl.ds(first, rows, stride=2),)]
    right = ref[index + (pl.ds(first + 1, rows, stride=2),)]
    return jnp.concatenate([left, right], axis=1)


def block(k):
    return slice(256 * k, 256 * k + 256)


RIGHT = (0, 768, 1280, 1536)
LEFT = (0, 0, 256, 768)


def right(k, j):
    return block(RIGHT[k] // 256 + j - k - 1)


def left(k, m):
    return block(LEFT[k] // 256 + m)


def corner_factors(place, lower_fill, upper_fill, mine, other, inv, vh, vl, wh, wl, ih, il):
    here_x, core = place[0], place[2]

    def corner(b, k):
        parts = []
        for i in range(4):
            at = (lax.rem(here_x - i + 4, 4), b // 2, k - (k > b))
            parts.append(jnp.where(core == b % 2, pair(mine, at, 64), pair(other, at, 64)))
        return jnp.concatenate(parts, axis=0)

    for k in range(4):
        ih[k], il[k] = split(inv[k])
    low, high = {}, {}
    for k in range(4):
        for m in range(k):
            t = dot3(split(corner(k, m)), (ih[m], il[m]))
            for n in range(m):
                t = t - dot3(low[k, n], (vh[:, right(n, m)], vl[:, right(n, m)]))
            keep = (lower_fill[m, k] == 1).astype(jnp.float32)
            low[k, m] = split(t * keep)
            wh[:, left(k, m)], wl[:, left(k, m)] = low[k, m]
        for j in range(k + 1, 4):
            t = corner(k, j)
            for m in range(k):
                t = t - dot3(low[k, m], high[m, j])
            keep = (upper_fill[k, j] == 1).astype(jnp.float32)
            high[k, j] = split(t * keep)
            t = dot3(high[k, j], (ih[j], il[j]))
            vh[:, right(k, j)], vl[:, right(k, j)] = split(t)


def scale_kernel(panels, inv, out):
    for k in range(4):
        out[:, block(k)] = dot3(split(pair(panels, (0, k), 384)), split(inv[k]))


def update_kernel(
    place, lower_fill, upper_fill, scaled, p0, p1, p2, mine, other, mine_c, other_c, inv,
    out, acc, lh, ll, uh, ul, vh, vl, wh, wl, ih, il, rows, sem
):
    core, here_col, here_row = place[2], place[3], place[4]

    @pl.when(pl.program_id(0) == 0)
    def _():
        copies = [
            pltpu.make_async_copy(mine, rows.at[:, core], sem.at[0]),
            pltpu.make_async_copy(other, rows.at[:, 1 - core], sem.at[1]),
        ]
        for copy in copies:
            copy.start()
        corner_factors(
            place, lower_fill, upper_fill, mine_c, other_c, inv, vh, vl, wh, wl, ih, il
        )
        for copy in copies:
            copy.wait()
        for k in range(4):
            before = slice(0, 256 * k)
            lefts = slice(LEFT[k], LEFT[k] + 256 * k)
            for c in range(3):
                t = pair(rows, (k // 2, k % 2), 256, 512 * c)
                if k:
                    t = t - dot3(
                        (wh[:, lefts], wl[:, lefts]), (uh[before, block(c)], ul[before, block(c)])
                    )
                j = c * 16 + here_col
                keep = ((j > k) & (upper_fill[k, j] == 1)).astype(jnp.float32)
                uh[block(k), block(c)], ul[block(k), block(c)] = split(t * keep)

    blocks = [g * 8 + here_row for g in range(6)]
    for k in range(4):
        src = acc if k else scaled
        for g, b in enumerate(blocks):
            here = slice(64 * g, 64 * g + 64)
            keep = ((b > k) & (lower_fill[k, b] == 1)).astype(jnp.float32)
            t = src[here, block(k)] * keep
            acc[here, block(k)] = t
            lh[here, block(k)], ll[here, block(k)] = split(t)
        if k < 3:
            after = slice(256 * k + 256, 1024)
            rights = slice(RIGHT[k], RIGHT[k + 1])
            t = dot3((lh[:, block(k)], ll[:, block(k)]), (vh[:, rights], vl[:, rights]))
            acc[:, after] = src[:, after] - t
    own = pl.ds(pl.multiple_of(jnp.minimum(here_col, 3) * 256, 256), 256)
    for c in range(3):
        t = dot3((lh[...], ll[...]), (uh[:, block(c)], ul[:, block(c)]))
        for g in range(6):
            here = slice(64 * g, 64 * g + 64)
            new = pair((p0, p1, p2)[c], (g, 0), 64) - t[here]
            if c == 0:
                new = jnp.where((here_col < 4) & (blocks[g] > here_col), acc[here, own], new)
            out[g, 0, pl.ds(2 * c, 64, stride=6), :] = new[:, :128]
            out[g, 0, pl.ds(2 * c + 1, 64, stride=6), :] = new[:, 128:]


def whole(*shape):
    return pl.BlockSpec(shape, lambda i: (0,) * len(shape))


def scatter_x(blocks):
    return [
        lax.ppermute(blocks[s], "pcol", [(k, k + 4 * s) for k in range(4)]) for s in range(1, 4)
    ]


def scattered(block, got, here_x):
    return jnp.where(here_x == 0, block, got[0] + got[1] + got[2])


def hop_z(value, pairs):
    return lax.ppermute(value, "prow", [(2 * a + c, 2 * b + c) for a, b in pairs for c in (0, 1)])


def spread_z(top, hops, here_z):
    away, near = hops
    on = hop_z(away, [(3, 2), (2, 3)])
    d0 = jnp.where(here_z == 0, top, jnp.where(here_z == 1, near, jnp.where(here_z == 2, on, away)))
    d1 = jnp.where(here_z == 1, top, jnp.where(here_z == 0, near, jnp.where(here_z == 3, on, away)))
    return jnp.stack([d0, d1])


def with_other(mine):
    return mine, lax.ppermute(mine, "prow", [(p, p ^ 1) for p in range(8)])


def first_hops(top):
    return hop_z(top, [(0, 3), (1, 2)]), hop_z(top, [(0, 1), (1, 0)])


def body(matrix, row_order, inverses, lower_fill, upper_fill):
    here_row = lax.axis_index("prow")
    here_col = lax.axis_index("pcol")
    here_x, here_y = here_col // 4, here_col % 4
    here_z, core = here_row // 2, here_row % 2
    x = matrix.reshape(4608, 2, 128)
    targets = row_order.reshape(6, 8, 256)
    local = jnp.arange(1536, dtype=jnp.int32)

    def keys(t):
        owner, row = t // 256 % 8, t // 2048 * 256 + t % 256
        return (owner * 2048 + local) * 2048 + row

    mine = lax.dynamic_slice(targets, (0, here_row, 0), (6, 1, 256)).reshape(12, 128)
    s0, slots = send_first(mine, x)
    s1, s2 = send_rest(slots, x)
    a2a = lambda s: lax.all_to_all(s.reshape(8, -1, 128), "prow", 0, 0, tiled=True)
    g0 = a2a(s0).reshape(1536, 2, 128)
    all_keys = lax.sort(keys(targets.transpose(1, 0, 2).reshape(8, 1536)), dimension=1)
    places = lax.dynamic_slice(all_keys, (0, here_row * 192), (8, 192)).reshape(1536) % 2048
    backward = lax.sort(places * 2048 + local) % 2048
    p0 = place_rows(backward, g0)
    p0, s1 = lax.optimization_barrier((p0, s1))
    g1, g2 = [a2a(s).reshape(1536, 2, 128) for s in (s1, s2)]
    parts0 = p0.reshape(6, 4, 128, 128)
    got, g1 = lax.optimization_barrier((scatter_x([parts0[:, i] for i in range(4)]), g1))
    quarter = scattered(parts0[:, 0], got, here_x)
    panels = lax.all_gather(quarter.reshape(768, 128), "pcol", axis=0, tiled=True)
    panels = panels.reshape(4, 4, 768, 128)
    p1 = place_rows(backward, g1)
    along_y = lambda s: [(q, q // 4 * 4 + (q + s) % 4) for q in range(16)]
    along_x = lambda s: [(q, (q + 4 * s) % 16) for q in range(16)]
    shifts = lambda v, along: [lax.ppermute(v, "pcol", along(s)) for s in (1, 2, 3)]
    corner, p1 = lax.optimization_barrier((jnp.stack([quarter[0]] + shifts(quarter[0], along_y)), p1))
    place = jnp.stack([here_x, here_y, core, here_col, here_row]).astype(jnp.int32)
    corner = pl.pallas_call(
        corner_rows_kernel,
        out_shape=f32(3, 128, 128),
        in_specs=[SMEM, VMEM],
        out_specs=VMEM,
        compiler_params=PARAMS,
        name="corner_rows",
    )(place, corner)
    hops, g2 = lax.optimization_barrier((first_hops(corner), g2))
    corner = spread_z(corner, hops, here_z)
    top = top_rows(backward[:256], p0, p1, g2).reshape(1536, 128)
    corner, top = lax.optimization_barrier((corner, top))
    rows = with_other(spread_z(top, first_hops(top), here_z))
    p2 = place_rows(backward, g2)
    corner, panels, p2 = lax.optimization_barrier((corner, panels, p2))
    scaled = pl.pallas_call(
        scale_kernel,
        out_shape=f32(1536, 1024),
        grid=(4,),
        in_specs=[pl.BlockSpec((1, 4, 768, 128), lambda i: (i, 0, 0, 0)), whole(4, 256, 256)],
        out_specs=pl.BlockSpec((384, 1024), lambda i: (i, 0)),
        compiler_params=PARAMS,
        name="scale",
    )(panels, inverses)
    far, scaled = lax.optimization_barrier((shifts(corner, along_x), scaled))
    corner = with_other(jnp.stack([corner] + far))
    part = lambda n: pl.BlockSpec((6, 1, n, 128), lambda i: (0, i, 0, 0))
    out = pl.pallas_call(
        update_kernel,
        out_shape=f32(6, 4, 384, 128),
        grid=(4,),
        in_specs=[SMEM] * 3
        + [pl.BlockSpec((384, 1024), lambda i: (i, 0))]
        + [part(128)] * 3
        + [pl.BlockSpec(memory_space=pl.ANY)] * 2
        + [whole(4, 2, 3, 128, 128)] * 2
        + [whole(4, 256, 256)],
        out_specs=part(384),
        scratch_shapes=[
            pltpu.VMEM((384, 1024), jnp.float32),
            pltpu.VMEM((384, 1024), BF),
            pltpu.VMEM((384, 1024), BF),
        ]
        + [pltpu.VMEM((1024, 768), BF)] * 2
        + [pltpu.VMEM((256, 1536), BF)] * 4
        + [pltpu.VMEM((4, 256, 256), BF)] * 2
        + [pltpu.VMEM((2, 2, 1536, 128), jnp.float32), pltpu.SemaphoreType.DMA((2,))],
        compiler_params=LARGE,
        name="update",
    )(
        place, lower_fill, upper_fill, scaled,
        *[p.reshape(6, 4, 128, 128) for p in (p0, p1, p2)], *rows, *corner, inverses
    )
    return out.reshape(6, 1, 256, 3, 1, 256)


def solution(mesh):
    in_specs = (P(None, "prow", None, None, "pcol", None), P(), P(), P(), P())
    out_specs = P(None, "prow", None, None, "pcol", None)
    return jax.shard_map(body, mesh=mesh, in_specs=in_specs, out_specs=out_specs, check_vma=False)
```

```python
import jax
import jax.numpy as jnp
from jax import lax
from jax.experimental import pallas as pl
from jax.experimental.pallas import tpu as pltpu
from jax.sharding import PartitionSpec as P

VMEM = pl.BlockSpec(memory_space=pltpu.VMEM)
SMEM = pl.BlockSpec(memory_space=pltpu.SMEM)
PARAMS = pltpu.CompilerParams(vmem_limit_bytes=14 * 1024 * 1024)
LARGE = pltpu.CompilerParams(vmem_limit_bytes=40 * 1024 * 1024)
BF = jnp.bfloat16


def f32(*shape):
    return jax.ShapeDtypeStruct(shape, jnp.float32)


def b16(*shape):
    return jax.ShapeDtypeStruct(shape, BF)


def split(t):
    high = t.astype(BF)
    return high, (t - high.astype(jnp.float32)).astype(BF)


def dot3(a, b):
    dot = lambda u, v: jnp.dot(u, v, preferred_element_type=jnp.float32)
    return dot(a[0], b[0]) + (dot(a[0], b[1]) + dot(a[1], b[0]))


def first_kernel(targets, x, out, slots, spots, sem):
    @pl.when(pl.program_id(0) == 0)
    def _():
        owner = lax.rem(lax.div(targets[...], 256), 8)
        hot = jnp.concatenate([(owner == d).astype(jnp.float32) for d in range(8)], axis=0)
        r = lax.broadcasted_iota(jnp.int32, (128, 128), 0)
        c = lax.broadcasted_iota(jnp.int32, (128, 128), 1)
        ahead = jnp.dot(hot, (r < c).astype(jnp.float32), preferred_element_type=jnp.float32)
        r = lax.broadcasted_iota(jnp.int32, (96, 96), 0)
        c = lax.broadcasted_iota(jnp.int32, (96, 96), 1)
        earlier = ((c < r) & (lax.div(r, 12) == lax.div(c, 12))).astype(jnp.float32)
        total = jnp.broadcast_to(jnp.sum(hot, axis=1, keepdims=True), (96, 128))
        ahead = ahead + jnp.dot(earlier, total, preferred_element_type=jnp.float32)
        slot = jnp.zeros((12, 128), jnp.float32)
        for d in range(8):
            part = slice(12 * d, 12 * d + 12)
            slot = slot + hot[part] * (ahead[part] + 192.0 * d)
        slots[...] = slot.astype(jnp.int32)
        copy = pltpu.make_async_copy(slots, spots, sem)
        copy.start()
        copy.wait()

    base = pl.program_id(0) * 3

    def step(j, carry):
        for q in range(3):
            out[spots[base + q, j]] = x[384 * q + 3 * j]
        return carry

    lax.fori_loop(0, 128, step, 0, unroll=4)


def send_first(targets, x):
    return pl.pallas_call(
        first_kernel,
        out_shape=(f32(1536, 2, 128), jax.ShapeDtypeStruct((12, 128), jnp.int32)),
        grid=(4,),
        in_specs=[
            pl.BlockSpec((12, 128), lambda i: (0, 0)),
            pl.BlockSpec((1152, 2, 128), lambda i: (i, 0, 0)),
        ],
        out_specs=(
            pl.BlockSpec((1536, 2, 128), lambda i: (0, 0, 0)),
            pl.BlockSpec((12, 128), lambda i: (0, 0)),
        ),
        scratch_shapes=[pltpu.SMEM((12, 128), jnp.int32), pltpu.SemaphoreType.DMA],
        compiler_params=PARAMS,
        name="send_first",
    )(targets, x)


def rest_kernel(slots, x, second, third):
    base = pl.program_id(0) * 3

    def step(j, carry):
        for q in range(3):
            d, r = slots[base + q, j], 384 * q + 3 * j
            second[d] = x[r + 1]
            third[d] = x[r + 2]
        return carry

    lax.fori_loop(0, 128, step, 0, unroll=4)


def send_rest(slots, x):
    return pl.pallas_call(
        rest_kernel,
        out_shape=[f32(1536, 2, 128)] * 2,
        grid=(4,),
        in_specs=[SMEM, pl.BlockSpec((1152, 2, 128), lambda i: (i, 0, 0))],
        out_specs=[pl.BlockSpec((1536, 2, 128), lambda i: (0, 0, 0))] * 2,
        compiler_params=PARAMS,
        name="send_rest",
    )(slots, x)


def top_kernel(order, p0, p1, arrived, out):
    out[:256] = p0[...]
    out[256:512] = p1[...]

    def step(d, carry):
        out[512 + d] = arrived[order[d]]
        return carry

    lax.fori_loop(0, 256, step, 0, unroll=8)


def top_rows(order, p0, p1, arrived):
    own = pl.BlockSpec((256, 2, 128), lambda i: (0, 0, 0))
    return pl.pallas_call(
        top_kernel,
        out_shape=f32(768, 2, 128),
        grid=(1,),
        in_specs=[SMEM, own, own, pl.BlockSpec((1536, 2, 128), lambda i: (0, 0, 0))],
        out_specs=pl.BlockSpec((768, 2, 128), lambda i: (0, 0, 0)),
        compiler_params=PARAMS,
        name="top_rows",
    )(order, p0, p1, arrived)


def place_kernel(order, arrived, out):
    def step(d, carry):
        out[d] = arrived[order[d]]
        return carry

    lax.fori_loop(0, 1536, step, 0, unroll=8)


def place_rows(order, arrived):
    return pl.pallas_call(
        place_kernel,
        out_shape=f32(*arrived.shape),
        in_specs=[SMEM, VMEM],
        out_specs=VMEM,
        compiler_params=PARAMS,
        name="place_rows",
    )(order, arrived)


def corner_rows_kernel(place, pieces, out):
    here_y, here_row = place[1], place[4]
    for j in range(3):
        k = j + (here_row <= j).astype(jnp.int32)
        out[j] = pieces[lax.rem(here_y - k + 4, 4)]


def pair(ref, index, rows, first=0):
    left = ref[index + (pl.ds(first, rows, stride=2),)]
    right = ref[index + (pl.ds(first + 1, rows, stride=2),)]
    return jnp.concatenate([left, right], axis=1)


def block(k):
    return slice(256 * k, 256 * k + 256)


RIGHT = (0, 768, 1280, 1536)
LEFT = (0, 0, 256, 768)


def right(k, j):
    return block(RIGHT[k] // 256 + j - k - 1)


def left(k, m):
    return block(LEFT[k] // 256 + m)


def corner_factors(place, lower_fill, upper_fill, mine, other, inv, vh, vl, wh, wl, ih, il):
    here_x, core = place[0], place[2]

    def corner(b, k):
        parts = []
        for i in range(4):
            at = (lax.rem(here_x - i + 4, 4), b // 2, k - (k > b))
            parts.append(jnp.where(core == b % 2, pair(mine, at, 64), pair(other, at, 64)))
        return jnp.concatenate(parts, axis=0)

    for k in range(4):
        ih[k], il[k] = split(inv[k])
    low, high = {}, {}
    for k in range(4):
        for m in range(k):
            t = dot3(split(corner(k, m)), (ih[m], il[m]))
            for n in range(m):
                t = t - dot3(low[k, n], (vh[:, right(n, m)], vl[:, right(n, m)]))
            keep = (lower_fill[m, k] == 1).astype(jnp.float32)
            low[k, m] = split(t * keep)
            wh[:, left(k, m)], wl[:, left(k, m)] = low[k, m]
        for j in range(k + 1, 4):
            t = corner(k, j)
            for m in range(k):
                t = t - dot3(low[k, m], high[m, j])
            keep = (upper_fill[k, j] == 1).astype(jnp.float32)
            high[k, j] = split(t * keep)
            t = dot3(high[k, j], (ih[j], il[j]))
            vh[:, right(k, j)], vl[:, right(k, j)] = split(t)


def scale_kernel(panels, inv, out):
    for k in range(4):
        out[:, block(k)] = dot3(split(pair(panels, (0, k), 384)), split(inv[k]))


def update_kernel(
    place, lower_fill, upper_fill, scaled, p0, p1, p2, mine, other, mine_c, other_c, inv,
    out, acc, lh, ll, uh, ul, vh, vl, wh, wl, ih, il
):
    core, here_col, here_row = place[2], place[3], place[4]

    @pl.when(pl.program_id(0) == 0)
    def _():
        corner_factors(
            place, lower_fill, upper_fill, mine_c, other_c, inv, vh, vl, wh, wl, ih, il
        )
        for k in range(4):
            before = slice(0, 256 * k)
            lefts = slice(LEFT[k], LEFT[k] + 256 * k)
            for c in range(3):
                at, first = (k // 2,), 512 * c
                t = jnp.where(
                    core == k % 2, pair(mine, at, 256, first), pair(other, at, 256, first)
                )
                if k:
                    t = t - dot3(
                        (wh[:, lefts], wl[:, lefts]), (uh[before, block(c)], ul[before, block(c)])
                    )
                j = c * 16 + here_col
                keep = ((j > k) & (upper_fill[k, j] == 1)).astype(jnp.float32)
                uh[block(k), block(c)], ul[block(k), block(c)] = split(t * keep)

    group = lax.broadcasted_iota(jnp.int32, (384, 1), 0) // 64

    def per_row(values):
        t = values[5]
        for g in range(5):
            t = jnp.where(group == g, values[g], t)
        return t

    blocks = [g * 8 + here_row for g in range(6)]
    for k in range(4):
        keep = [((b > k) & (lower_fill[k, b] == 1)).astype(jnp.float32) for b in blocks]
        t = (acc if k else scaled)[:, block(k)] * per_row(keep)
        acc[:, block(k)] = t
        high, low = split(t)
        lh[:, block(k)], ll[:, block(k)] = high, low
        if k < 3:
            after = slice(256 * k + 256, 1024)
            rights = slice(RIGHT[k], RIGHT[k + 1])
            t = dot3((high, low), (vh[:, rights], vl[:, rights]))
            acc[:, after] = (acc if k else scaled)[:, after] - t
    done = (here_col < 4) & (per_row(blocks) > here_col)
    own = pl.ds(pl.multiple_of(jnp.minimum(here_col, 3) * 256, 256), 256)
    for c in range(3):
        t = dot3((lh[...], ll[...]), (uh[:, block(c)], ul[:, block(c)]))
        for g in range(6):
            here = slice(64 * g, 64 * g + 64)
            new = pair((p0, p1, p2)[c], (g, 0), 64) - t[here]
            if c == 0:
                new = jnp.where(done[here], acc[here, own], new)
            out[g, 0, pl.ds(2 * c, 64, stride=6), :] = new[:, :128]
            out[g, 0, pl.ds(2 * c + 1, 64, stride=6), :] = new[:, 128:]


def whole(*shape):
    return pl.BlockSpec(shape, lambda i: (0,) * len(shape))


def scatter_x(blocks):
    return [
        lax.ppermute(blocks[s], "pcol", [(k, k + 4 * s) for k in range(4)]) for s in range(1, 4)
    ]


def scattered(block, got, here_x):
    return jnp.where(here_x == 0, block, got[0] + got[1] + got[2])


def hop_z(value, pairs):
    return lax.ppermute(value, "prow", [(2 * a + c, 2 * b + c) for a, b in pairs for c in (0, 1)])


def spread_z(top, hops, here_z):
    away, near = hops
    on = hop_z(away, [(3, 2), (2, 3)])
    d0 = jnp.where(here_z == 0, top, jnp.where(here_z == 1, near, jnp.where(here_z == 2, on, away)))
    d1 = jnp.where(here_z == 1, top, jnp.where(here_z == 0, near, jnp.where(here_z == 3, on, away)))
    return jnp.stack([d0, d1])


def with_other(mine):
    return mine, lax.ppermute(mine, "prow", [(p, p ^ 1) for p in range(8)])


def first_hops(top):
    return hop_z(top, [(0, 3), (1, 2)]), hop_z(top, [(0, 1), (1, 0)])


def body(matrix, row_order, inverses, lower_fill, upper_fill):
    here_row = lax.axis_index("prow")
    here_col = lax.axis_index("pcol")
    here_x, here_y = here_col // 4, here_col % 4
    here_z, core = here_row // 2, here_row % 2
    x = matrix.reshape(4608, 2, 128)
    targets = row_order.reshape(6, 8, 256)
    local = jnp.arange(1536, dtype=jnp.int32)

    def keys(t):
        owner, row = t // 256 % 8, t // 2048 * 256 + t % 256
        return (owner * 2048 + local) * 2048 + row

    mine = lax.dynamic_slice(targets, (0, here_row, 0), (6, 1, 256)).reshape(12, 128)
    s0, slots = send_first(mine, x)
    s1, s2 = send_rest(slots, x)
    a2a = lambda s: lax.all_to_all(s.reshape(8, -1, 128), "prow", 0, 0, tiled=True)
    g0 = a2a(s0).reshape(1536, 2, 128)
    all_keys = lax.sort(keys(targets.transpose(1, 0, 2).reshape(8, 1536)), dimension=1)
    places = lax.dynamic_slice(all_keys, (0, here_row * 192), (8, 192)).reshape(1536) % 2048
    backward = lax.sort(places * 2048 + local) % 2048
    p0 = place_rows(backward, g0)
    p0, s1 = lax.optimization_barrier((p0, s1))
    g1, g2 = [a2a(s).reshape(1536, 2, 128) for s in (s1, s2)]
    parts0 = p0.reshape(6, 4, 128, 128)
    got, g1 = lax.optimization_barrier((scatter_x([parts0[:, i] for i in range(4)]), g1))
    quarter = scattered(parts0[:, 0], got, here_x)
    panels = lax.all_gather(quarter.reshape(768, 128), "pcol", axis=0, tiled=True)
    panels = panels.reshape(4, 4, 768, 128)
    p1 = place_rows(backward, g1)
    along_y = lambda s: [(q, q // 4 * 4 + (q + s) % 4) for q in range(16)]
    along_x = lambda s: [(q, (q + 4 * s) % 16) for q in range(16)]
    shifts = lambda v, along: [lax.ppermute(v, "pcol", along(s)) for s in (1, 2, 3)]
    corner, p1 = lax.optimization_barrier((jnp.stack([quarter[0]] + shifts(quarter[0], along_y)), p1))
    place = jnp.stack([here_x, here_y, core, here_col, here_row]).astype(jnp.int32)
    corner = pl.pallas_call(
        corner_rows_kernel,
        out_shape=f32(3, 128, 128),
        in_specs=[SMEM, VMEM],
        out_specs=VMEM,
        compiler_params=PARAMS,
        name="corner_rows",
    )(place, corner)
    hops, g2 = lax.optimization_barrier((first_hops(corner), g2))
    corner = spread_z(corner, hops, here_z)
    top = top_rows(backward[:256], p0, p1, g2).reshape(1536, 128)
    corner, top = lax.optimization_barrier((corner, top))
    rows = with_other(spread_z(top, first_hops(top), here_z))
    p2 = place_rows(backward, g2)
    corner, panels, p2 = lax.optimization_barrier((corner, panels, p2))
    scaled = pl.pallas_call(
        scale_kernel,
        out_shape=f32(1536, 1024),
        grid=(4,),
        in_specs=[pl.BlockSpec((1, 4, 768, 128), lambda i: (i, 0, 0, 0)), whole(4, 256, 256)],
        out_specs=pl.BlockSpec((384, 1024), lambda i: (i, 0)),
        compiler_params=PARAMS,
        name="scale",
    )(panels, inverses)
    corner = with_other(jnp.stack([corner] + shifts(corner, along_x)))
    part = lambda n: pl.BlockSpec((6, 1, n, 128), lambda i: (0, i, 0, 0))
    out = pl.pallas_call(
        update_kernel,
        out_shape=f32(6, 4, 384, 128),
        grid=(4,),
        in_specs=[SMEM] * 3
        + [pl.BlockSpec((384, 1024), lambda i: (i, 0))]
        + [part(128)] * 3
        + [whole(2, 1536, 128)] * 2
        + [whole(4, 2, 3, 128, 128)] * 2
        + [whole(4, 256, 256)],
        out_specs=part(384),
        scratch_shapes=[
            pltpu.VMEM((384, 1024), jnp.float32),
            pltpu.VMEM((384, 1024), BF),
            pltpu.VMEM((384, 1024), BF),
        ]
        + [pltpu.VMEM((1024, 768), BF)] * 2
        + [pltpu.VMEM((256, 1536), BF)] * 4
        + [pltpu.VMEM((4, 256, 256), BF)] * 2,
        compiler_params=LARGE,
        name="update",
    )(
        place, lower_fill, upper_fill, scaled,
        *[p.reshape(6, 4, 128, 128) for p in (p0, p1, p2)], *rows, *corner, inverses
    )
    return out.reshape(6, 1, 256, 3, 1, 256)


def solution(mesh):
    in_specs = (P(None, "prow", None, None, "pcol", None), P(), P(), P(), P())
    out_specs = P(None, "prow", None, None, "pcol", None)
    return jax.shard_map(body, mesh=mesh, in_specs=in_specs, out_specs=out_specs, check_vma=False)
```
